32 devices in a mesh: groups: 2 (over y), gz: 4 (over z), gy: 2 (over x), gx: 2 (over core).
Axes of the slice: x: 2, y: 2, z: 4, core: 2. Of those that a mesh axis runs over, the one named last changes fastest.
Arguments:
- density: float32 [72, 20, 244], P(('groups', 'gz'), 'gy', 'gx'), parts along dimension 0, may hold values from 2 to 4
- momentum: float32 [3, 72, 20, 244], P(None, ('groups', 'gz'), 'gy', 'gx'), parts along dimension 1, may hold values from -1 to 1
- energy: float32 [72, 20, 244], P(('groups', 'gz'), 'gy', 'gx'), parts along dimension 0, may hold values from 4 to 8
- cotangent: float32 [5, 72, 20, 244], P(None, ('groups', 'gz'), 'gy', 'gx'), parts along dimension 1, may hold values from -6 to 6
- bc_codes: int32 [8], P('groups'), parts along dimension 0, may hold values from 0 to 1, as said below
- weight_in: float32 [3, 16], replicated, may hold values from -6 to 6
- weight_out: float32 [16, 3], replicated, may hold values from -6 to 6
Outputs:
- new_state: float32 [5, 72, 20, 244], P(None, ('groups', 'gz'), 'gy', 'gx'), parts along dimension 1
- state_grad: float32 [5, 72, 20, 244], P(None, ('groups', 'gz'), 'gy', 'gx'), parts along dimension 1
The draws below stay inside these ranges and needn't reach their ends.
There are 2 independent parts, one for each index of `groups`. The reference program is written for one: setup_inputs(seed, part) draws one part's arguments, and reference() takes and returns one part's arrays. A program takes and returns all parts, laid end to end along the dimension named above; an argument that names none is the same for every part. Nothing has to cross between parts.
Inputs may be any that keep to these rules, and one draw needn't show every extreme that they name: `bc_codes`: 0 marks a reflecting wall, 1 a zero-gradient outflow; exactly two of the four faces are walls.
All inputs are finite; a program needn't handle non-finite values.
Results may differ from the reference program's by a relative error of at most 0.0003.
Values sent between devices are 32-bit elements; how exact they have to be, the bound alone decides.
A program may use at most 320 MiB of HBM per device.

```python
import math
import jax
import jax.numpy as jnp
from jax import lax

CZ = 9
HID = 16
NX = 244
NY = 20
NZ = 36


def draw_bc_codes(key, part):
    key = jax.random.fold_in(key, 7)
    return (jax.random.permutation(key, 4) % 2).astype(jnp.int32)


def block_levels(own_key, shape, split, least, largest):
    level = 1.0
    for dim, shards_of in split:
        steps = jax.random.uniform(jax.random.fold_in(jax.random.fold_in(own_key, 6), dim), (shards_of,), jnp.float32, least / len(split), largest / len(split))
        level = level * jnp.repeat(jnp.exp(steps), shape[dim] // shards_of).reshape((-1,) + (1,) * (len(shape) - 1 - dim))
    return level


def bell_draw(own_key, dims, deviation, most, split=(), kind=jnp.bfloat16):
    values = jax.random.normal(own_key, dims, jnp.float32) * deviation
    if len(split) > 0:
        values = block_levels(own_key, dims, split, -0.22, 0.18) * values
    return jnp.clip(values, min=-most, max=most).astype(kind)


def setup_inputs(seed: int = 0, part: int = 0) -> dict:
    seeds = jax.random.split(jax.random.key(seed), 8)
    part_splits = jax.random.split(jax.random.fold_in(seeds[7], part), 8)
    return {
        "density": jnp.clip(jnp.exp(math.log(4.0) - 0.6931472 * jax.random.uniform(part_splits[0], (NZ, NY, NX), jnp.float32) ** block_levels(part_splits[0], (NZ, NY, NX), ((0, 4), (1, 2), (2, 2)), -0.2, 0.2)), 2.0, 4.0),
        "momentum": bell_draw(part_splits[1], (3, NZ, NY, NX), 0.25, 1.0, ((1, 4), (2, 2), (3, 2)), jnp.float32),
        "energy": jnp.clip(4.0 + 4.0 * jax.random.uniform(part_splits[2], (NZ, NY, NX), jnp.float32) ** block_levels(part_splits[2], (NZ, NY, NX), ((0, 4), (1, 2), (2, 2)), -0.2, 0.2), 4.0, 8.0),
        "cotangent": bell_draw(part_splits[3], (5, NZ, NY, NX), 1.0, 6.0, ((1, 4), (2, 2), (3, 2)), jnp.float32),
        "bc_codes": draw_bc_codes(jax.random.fold_in(jax.random.fold_in(seeds[7], part), 71), part),
        "weight_in": bell_draw(seeds[5], (3, HID), 1.5, 6.0, (), jnp.float32),
        "weight_out": bell_draw(seeds[6], (HID, 3), 1.5, 6.0, (), jnp.float32),
    }


time_step = 0.06
split_speed = 2.0
viscosity = 0.02
conduction = 0.03

def take_cells(field, start, length, axis):
    return lax.slice_in_dim(field, start, start + length, axis=axis)

def face_value(stencil, weight_in, weight_out):
    first, second, third, fourth, fifth = stencil
    polys = [(2.0 * first - 7.0 * second + 11.0 * third) / 6.0, (-second + 5.0 * third + 2.0 * fourth) / 6.0, (2.0 * third + 5.0 * fourth - fifth) / 6.0]
    curve_a = first - 2.0 * second + third
    slope_a = first - 4.0 * second + 3.0 * third
    curve_b = second - 2.0 * third + fourth
    slope_b = second - fourth
    curve_c = third - 2.0 * fourth + fifth
    slope_c = 3.0 * third - 4.0 * fourth + fifth
    smooth = [13.0 / 12.0 * curve_a * curve_a + 0.25 * slope_a * slope_a, 13.0 / 12.0 * curve_b * curve_b + 0.25 * slope_b * slope_b, 13.0 / 12.0 * curve_c * curve_c + 0.25 * slope_c * slope_c]
    total = smooth[0] + smooth[1] + smooth[2] + 0.1
    feats = jnp.stack([lax.optimization_barrier(jnp.mean(piece / total, axis=0)) for piece in smooth], 0)
    hidden = jnp.tanh(jnp.einsum('kh,kabc->habc', weight_in, feats, precision=lax.Precision.HIGHEST))
    scores = jnp.einsum('hk,habc->kabc', weight_out, hidden, precision=lax.Precision.HIGHEST)
    linear = jnp.array([0.1, 0.6, 0.3], jnp.float32).reshape(3, 1, 1, 1)
    gated = (jax.nn.softplus(scores) + 0.05) * linear
    weights = gated / lax.optimization_barrier(jnp.sum(gated, axis=0, keepdims=True))
    return weights[0:1] * polys[0] + weights[1:2] * polys[1] + weights[2:3] * polys[2]

def direction_term(line, axis, comp, weight_in, weight_out):
    cells = line.shape[axis] - 6
    dens = line[0:1]
    moment = line[1:4]
    energy_line = line[4:5]
    inverse = 1.0 / dens
    veloc = moment * inverse
    press = 0.4 * (energy_line - 0.5 * lax.optimization_barrier(jnp.sum(moment * veloc, axis=0, keepdims=True)))
    normal_vel = veloc[comp - 1:comp]
    unit = (jnp.arange(3) == comp - 1).astype(line.dtype).reshape(3, 1, 1, 1)
    flux = jnp.concatenate([moment[comp - 1:comp], moment * normal_vel + press * unit, (energy_line + press) * normal_vel], 0)
    plus = 0.5 * (flux + split_speed * line)
    minus = 0.5 * (flux - split_speed * line)
    faces = cells + 1
    face_flux = face_value([take_cells(plus, k, faces, axis) for k in range(5)], weight_in, weight_out)
    face_flux = face_flux + face_value([take_cells(minus, 5 - k, faces, axis) for k in range(5)], weight_in, weight_out)
    tendency = take_cells(face_flux, 0, cells, axis) - take_cells(face_flux, 1, cells, axis)
    smooth_vars = jnp.concatenate([veloc, press * inverse], 0)
    laplace = take_cells(smooth_vars, 4, cells, axis) - 2.0 * take_cells(smooth_vars, 3, cells, axis) + take_cells(smooth_vars, 2, cells, axis)
    diffusion = jnp.concatenate([jnp.zeros_like(laplace[0:1]), viscosity * laplace[0:3], conduction * laplace[3:4]], 0)
    return tendency + diffusion

def fill_edges(line, axis, code_low, code_high, comp, low_on, high_on):
    cells = line.shape[axis]
    flips = jnp.where(jnp.arange(5) == comp, -1.0, 1.0).astype(line.dtype).reshape(5, 1, 1, 1)
    wall_low = jnp.flip(take_cells(line, 3, 3, axis), axis) * flips
    copy_low = jnp.concatenate([take_cells(line, 3, 1, axis)] * 3, axis)
    ghost_low = jnp.where(low_on, jnp.where(code_low == 0, wall_low, copy_low), take_cells(line, 0, 3, axis))
    wall_high = jnp.flip(take_cells(line, cells - 6, 3, axis), axis) * flips
    copy_high = jnp.concatenate([take_cells(line, cells - 4, 1, axis)] * 3, axis)
    ghost_high = jnp.where(high_on, jnp.where(code_high == 0, wall_high, copy_high), take_cells(line, cells - 3, 3, axis))
    return jnp.concatenate([ghost_low, take_cells(line, 3, cells - 6, axis), ghost_high], axis)

def section_rhs(padded, codes, edges, weight_in, weight_out):
    line_z = padded[:, :, 3:-3, 3:-3]
    line_y = fill_edges(padded[:, 3:-3, :, 3:-3], 2, codes[0], codes[1], 2, edges[0], edges[1])
    line_x = fill_edges(padded[:, 3:-3, 3:-3, :], 3, codes[2], codes[3], 1, edges[2], edges[3])
    result = direction_term(line_z, 1, 3, weight_in, weight_out)
    result = result + direction_term(line_y, 2, 2, weight_in, weight_out)
    return result + direction_term(line_x, 3, 1, weight_in, weight_out)

def reference(density, momentum, energy, cotangent, bc_codes, weight_in, weight_out):
    state = jnp.concatenate([density[None], momentum, energy[None]], 0)
    edges = (True, True, True, True)

    def rhs_global(field):
        z_padded = jnp.pad(field, ((0, 0), (3, 3), (0, 0), (0, 0)), mode='wrap')
        padded = jnp.pad(z_padded, ((0, 0), (0, 0), (3, 3), (3, 3)))
        count = field.shape[1] // CZ

        def one_block(index):
            piece = lax.dynamic_slice_in_dim(padded, (index * CZ).astype(jnp.int32), CZ + 6, 1)
            return section_rhs(piece, bc_codes, edges, weight_in, weight_out)
        blocks = lax.map(jax.checkpoint(one_block), jnp.arange(count, dtype=jnp.int32))
        return jnp.transpose(blocks, (1, 0, 2, 3, 4)).reshape(field.shape)

    def step(field):
        section_one = field + time_step * rhs_global(field)
        section_two = 0.75 * field + 0.25 * (section_one + time_step * rhs_global(section_one))
        return 1.0 / 3.0 * field + 2.0 / 3.0 * (section_two + time_step * rhs_global(section_two))
    new_state, pullback = jax.vjp(step, state)
    return (new_state, pullback(cotangent)[0])
```

```python
import functools
import jax
import jax.numpy as jnp
from jax import lax
from jax.experimental import pallas as pl
from jax.experimental.pallas import tpu as pltpu
from jax.sharding import PartitionSpec as P

DT = 0.06
HID = 16
CZ, CY, CX = 9, 10, 122
ROWS = 96
LANES = 128
OWN = CZ * CY
FACE_ROWS = {"z": (0, 104, 104), "y": (208, 312, 104), "x": (416, 512, 96)}
FACES = 608
CELLS = 160
GPAD = 208
PITCH = {"z": 10, "y": 9}
COMP = {"z": 3, "y": 2, "x": 1}
W_IN = 12
W_OUT = 12 + 3 * HID


def roll(v, amount):
    return pltpu.roll(v, amount % LANES, 1)


def lane_mask(rows, low, high):
    lanes = lax.broadcasted_iota(jnp.int32, (rows, LANES), 1)
    return jnp.where((lanes >= low) & (lanes < high), 1.0, 0.0).astype(jnp.float32)


def cell_terms(comp, u):
    inverse = 1.0 / u[0]
    veloc = [u[i] * inverse for i in (1, 2, 3)]
    press = 0.4 * (u[4] - 0.5 * (u[1] * veloc[0] + u[2] * veloc[1] + u[3] * veloc[2]))
    normal = veloc[comp - 1]
    flux = [u[comp]]
    for i in (1, 2, 3):
        term = u[i] * normal
        flux.append(term + press if i == comp else term)
    flux.append((u[4] + press) * normal)
    return flux, veloc + [press * inverse]


def weno_unit(d, scal, grad, want_value):
    ratios, inverses = [], []
    feats = [0.0, 0.0, 0.0]
    for c in range(5):
        d1, d2, d3, d4 = d[0][c], d[1][c], d[2][c], d[3][c]
        b0 = 4.0 * d1 * d1 + d2 * (10.0 * d2 - 11.0 * d1)
        b1 = 4.0 * d3 * d3 + d2 * (4.0 * d2 - 5.0 * d3)
        b2 = 4.0 * d4 * d4 + d3 * (10.0 * d3 - 11.0 * d4)
        inv = 1.0 / (b0 + b1 + b2 + 0.3)
        r = [b0 * inv, b1 * inv, b2 * inv]
        ratios.append(r)
        inverses.append(inv)
        feats = [feats[k] + r[k] for k in range(3)]
    feats = [0.2 * f for f in feats]
    hidden = []
    for j in range(HID):
        pre = scal[W_IN + j] * feats[0]
        pre = pre + scal[W_IN + HID + j] * feats[1]
        pre = pre + scal[W_IN + 2 * HID + j] * feats[2]
        hidden.append(jnp.tanh(pre))
    linear = (0.1, 0.6, 0.3)
    gates, slopes = [], []
    for k in range(3):
        s = scal[W_OUT + k] * hidden[0]
        for j in range(1, HID):
            s = s + scal[W_OUT + 3 * j + k] * hidden[j]
        e = jnp.exp(-jnp.abs(s))
        gates.append(linear[k] * (jnp.maximum(s, 0.0) + jnp.log(1.0 + e) + 0.05))
        if grad is not None:
            slopes.append(linear[k] * jnp.where(s >= 0.0, 1.0, e) / (1.0 + e))
    inv_sum = 1.0 / (gates[0] + gates[1] + gates[2])
    w = [g * inv_sum for g in gates]
    a = [
        w[0] * (-1.0 / 3.0),
        (5.0 * w[0] + w[1]) * (1.0 / 6.0),
        (w[1] + 2.0 * w[2]) * (1.0 / 3.0),
        w[2] * (-1.0 / 6.0),
    ]
    value = None
    if want_value:
        value = [
            a[0] * d[0][c] + a[1] * d[1][c] + a[2] * d[2][c] + a[3] * d[3][c] for c in range(5)
        ]
    if grad is None:
        return value, None
    q = []
    for i in range(4):
        t = grad[0] * d[i][0]
        for c in range(1, 5):
            t = t + grad[c] * d[i][c]
        q.append(t * (1.0 / 6.0))
    dw = [5.0 * q[1] - 2.0 * q[0], q[1] + 2.0 * q[2], 4.0 * q[2] - q[3]]
    mid = w[0] * dw[0] + w[1] * dw[1] + w[2] * dw[2]
    ds = [(dw[k] - mid) * inv_sum * slopes[k] for k in range(3)]
    e = [0.0, 0.0, 0.0]
    for j in range(HID):
        dh = scal[W_OUT + 3 * j] * ds[0]
        dh = dh + scal[W_OUT + 3 * j + 1] * ds[1]
        dh = dh + scal[W_OUT + 3 * j + 2] * ds[2]
        dpre = dh * (1.0 - hidden[j] * hidden[j])
        e = [e[k] + scal[W_IN + HID * k + j] * dpre for k in range(3)]
    e = [0.2 * v for v in e]
    cells = [[], [], [], [], []]
    for c in range(5):
        d1, d2, d3, d4 = d[0][c], d[1][c], d[2][c], d[3][c]
        r, inv, gc = ratios[c], inverses[c], grad[c]
        m = e[0] * r[0] + e[1] * r[1] + e[2] * r[2]
        g0, g1, g2 = (e[0] - m) * inv, (e[1] - m) * inv, (e[2] - m) * inv
        dd1 = a[0] * gc + g0 * (8.0 * d1 - 11.0 * d2)
        dd2 = a[1] * gc + g0 * (20.0 * d2 - 11.0 * d1) + g1 * (8.0 * d2 - 5.0 * d3)
        dd3 = a[2] * gc + g1 * (8.0 * d3 - 5.0 * d2) + g2 * (20.0 * d3 - 11.0 * d4)
        dd4 = a[3] * gc + g2 * (8.0 * d4 - 11.0 * d3)
        cells[0].append(-dd1)
        cells[1].append(dd1 - dd2)
        cells[2].append(dd2 - dd3 + gc)
        cells[3].append(dd3 - dd4)
        cells[4].append(dd4)
    return value, cells


def build_lines(scal, q, zlo, zhi, ylo, yhi, xin, uz, uy, ux):
    for c in range(5):
        uz[c, 0:30] = zlo[c, 0:30]
        uz[c, 30:120] = q[c, 0:OWN]
        uz[c, 120:150] = zhi[c, 0:30]
        uz[c, 150:160] = jnp.ones((10, LANES), jnp.float32)
        for z in range(CZ):
            uy[c, pl.ds(27 + z, CY, stride=CZ), :] = q[c, z * CY : (z + 1) * CY]
        flip = -1.0 if c == 2 else 1.0
        for g in range(3):
            low = scal[0] * flip * uy[c, (5 - g) * 9 : (6 - g) * 9] + scal[1] * uy[c, 27:36]
            uy[c, g * 9 : g * 9 + 9] = low + scal[2] * ylo[c, g * 9 : g * 9 + 9]
            high = scal[3] * flip * uy[c, (12 - g) * 9 : (13 - g) * 9] + scal[4] * uy[c, 108:117]
            uy[c, (13 + g) * 9 : (14 + g) * 9] = high + scal[5] * yhi[c, g * 9 : g * 9 + 9]
        uy[c, 144:160] = jnp.ones((16, LANES), jnp.float32)
        flip = -1.0 if c == 1 else 1.0
        own = q[c]
        partner = xin[c]
        value = own * lane_mask(ROWS, 3, 125)
        low = scal[8] * roll(partner, 6)
        high = scal[11] * roll(partner, 122)
        value = value + lane_mask(ROWS, 0, 3) * low + lane_mask(ROWS, 125, 128) * high
        for g in range(3):
            at_low = lane_mask(ROWS, g, g + 1)
            value = value + at_low * (
                scal[6] * flip * roll(own, -(5 - 2 * g)) + scal[7] * roll(own, g - 3)
            )
            at_high = lane_mask(ROWS, 125 + g, 126 + g)
            value = value + at_high * (
                scal[9] * flip * roll(own, 1 + 2 * g) + scal[10] * roll(own, 1 + g)
            )
        ux[c] = value


def cell_loop(name, u, plus, minus, smooth, rows):
    def body(i, carry):
        at = pl.ds(pl.multiple_of(i * 8, 8), 8)
        cells = [u[c, at, :] for c in range(5)]
        flux, sv = cell_terms(COMP[name], cells)
        for c in range(5):
            plus[c, at, :] = 0.5 * flux[c] + cells[c]
            minus[c, at, :] = 0.5 * flux[c] - cells[c]
        if smooth is not None:
            for c in range(4):
                smooth[c, at, :] = sv[c]
        return carry

    lax.fori_loop(0, rows // 8, body, 0)


def spread_rows(name, plus, minus, diffs, base):
    p = PITCH[name]
    at_plus, at_minus, count = FACE_ROWS[name]
    for c in range(5):
        for start, size in ((0, 56), (56, 48)):
            f = [plus[c, start + k * p : start + k * p + size] for k in range(5)]
            for i in range(4):
                diffs[i, c, at_plus + start : at_plus + start + size] = f[i + 1] - f[i]
            middle = f[2]
            f = [minus[c, start + k * p : start + k * p + size] for k in range(1, 6)]
            for i in range(4):
                diffs[i, c, at_minus + start : at_minus + start + size] = f[3 - i] - f[4 - i]
            if base is not None:
                base[c, at_plus // 2 + start : at_plus // 2 + start + size] = middle + f[2]


def spread_lanes(plus, minus, diffs, base):
    at_plus, at_minus, count = FACE_ROWS["x"]
    for c in range(5):
        for start in (0, 48):
            v = plus[c, start : start + 48]
            diff = roll(v, -1) - v
            for i in range(4):
                diffs[i, c, at_plus + start : at_plus + start + 48] = roll(diff, -i)
            m = minus[c, start : start + 48]
            diff = m - roll(m, -1)
            for i in range(4):
                diffs[i, c, at_minus + start : at_minus + start + 48] = roll(diff, i - 4)
            if base is not None:
                base[c, at_plus // 2 + start : at_plus // 2 + start + 48] = roll(v, -2) + roll(
                    m, -3
                )


def lap_rows(name, smooth, out):
    p = PITCH[name]
    out[0] = jnp.zeros((ROWS, LANES), jnp.float32)
    for c in range(4):
        coef = 0.02 if c < 3 else 0.03
        s = [smooth[c, k * p : k * p + OWN] for k in (2, 3, 4)]
        out[c + 1, 0:OWN] = coef * (s[2] - 2.0 * s[1] + s[0])


def gather_grad(prev, coef, scale, own, zlo, zhi, ylo, yhi, xin, total, grad):
    for c in range(5):
        x = lane_mask(ROWS, 122, 125) * roll(xin[c], 122) + lane_mask(ROWS, 3, 6) * roll(xin[c], 6)
        total[c] = coef * prev[c] + own[c] + x
        total[c, 0:30] = total[c, 0:30] + zlo[c, 0:30]
        total[c, 60:90] = total[c, 60:90] + zhi[c, 0:30]
        for z in range(CZ):
            low = z * CY
            total[c, low : low + 3] = total[c, low : low + 3] + ylo[c, pl.ds(z, 3, stride=CZ), :]
            total[c, low + 7 : low + 10] = (
                total[c, low + 7 : low + 10] + yhi[c, pl.ds(z, 3, stride=CZ), :]
            )
        if grad is not None:
            grad[c] = scale * total[c]


def grad_faces(grad, gz, gy, dface):
    for c in range(5):
        gz[c] = jnp.zeros((GPAD, LANES), jnp.float32)
        gy[c] = jnp.zeros((GPAD, LANES), jnp.float32)
        gz[c, 40 : 40 + OWN] = grad[c, 0:OWN]
        for z in range(CZ):
            gy[c, pl.ds(36 + z, CY, stride=CZ), :] = grad[c, z * CY : (z + 1) * CY]
        dz = gz[c, 40:144] - gz[c, 30:134]
        dy = gy[c, 36:140] - gy[c, 27:131]
        g = grad[c]
        dx = roll(g, -3) - roll(g, -2)
        dface[c, 0:104] = dz
        dface[c, 104:208] = dz
        dface[c, 208:312] = dy
        dface[c, 312:416] = dy
        dface[c, 416:512] = dx
        dface[c, 512:608] = dx


def pull_rows(name, dcell, plus, minus, gpad, u, out):
    p = PITCH[name]
    at_plus, at_minus, count = FACE_ROWS[name]
    for c in range(5):
        plus[c] = jnp.zeros((CELLS, LANES), jnp.float32)
        minus[c] = jnp.zeros((CELLS, LANES), jnp.float32)
        for k in range(5):
            low = k * p
            plus[c, low : low + 104] = (
                plus[c, low : low + 104] + dcell[k, c, at_plus : at_plus + 104]
            )
            low = (5 - k) * p
            minus[c, low : low + 104] = (
                minus[c, low : low + 104] + dcell[k, c, at_minus : at_minus + 104]
            )
        if c > 0:
            coef = 0.02 if c < 4 else 0.03
            g = [gpad[c, k * p : k * p + CELLS] for k in range(3)]
            out[c] = coef * (g[0] - 2.0 * g[1] + g[2])
    pull_cells(name, plus, minus, u, out, CELLS)


def pull_lanes(dcell, plus, minus, grad, u, out):
    at_plus, at_minus, count = FACE_ROWS["x"]
    for c in range(5):
        sp = dcell[0, c, at_plus : at_plus + ROWS]
        sm = roll(dcell[0, c, at_minus : at_minus + ROWS], 5)
        for k in range(1, 5):
            sp = sp + roll(dcell[k, c, at_plus : at_plus + ROWS], k)
            sm = sm + roll(dcell[k, c, at_minus : at_minus + ROWS], 5 - k)
        plus[c, 0:ROWS] = sp
        minus[c, 0:ROWS] = sm
        if c > 0:
            coef = 0.02 if c < 4 else 0.03
            g = grad[c]
            out[c, 0:ROWS] = coef * (roll(g, 1) - 2.0 * g + roll(g, -1))
    pull_cells("x", plus, minus, u, out, ROWS)


def pull_cells(name, plus, minus, u, out, rows):
    def body(i, carry):
        at = pl.ds(pl.multiple_of(i * 8, 8), 8)
        cells = [u[c, at, :] for c in range(5)]
        dp = [plus[c, at, :] for c in range(5)]
        dm = [minus[c, at, :] for c in range(5)]
        dsv = [out[c, at, :] for c in range(1, 5)]
        unused, back = jax.vjp(functools.partial(cell_terms, COMP[name]), cells)
        (du,) = back(([0.5 * (dp[c] + dm[c]) for c in range(5)], dsv))
        for c in range(5):
            out[c, at, :] = du[c] + dp[c] - dm[c]
        return carry

    lax.fori_loop(0, rows // 8, body, 0)


def section_kernel(mode, consts, *refs):
    refs = list(refs)
    take = lambda n: [refs.pop(0) for _ in range(n)]
    (scal,) = take(1)
    q, zlo, zhi, ylo, yhi, xin = take(6)
    if mode != "back":
        (first,) = take(1)
    if mode == "both":
        (prev,) = take(1)
    if mode == "back":
        prev, own_in, gzlo, gzhi, gylo, gyhi, gxin = take(7)
    if mode != "back":
        (state_out,) = take(1)
    if mode == "fwd":
        szlo, szhi, sylo, syhi = take(4)
    if mode == "back":
        (total,) = take(1)
    if mode != "fwd":
        own_out, dzlo, dzhi, dylo, dyhi, dx = take(6)
    uz, uy, ux, plus, minus, smooth, diffs = take(7)
    if mode != "back":
        base, tend_z, tend_y, tend_x, corr = take(5)
    else:
        base = None
    if mode != "fwd":
        grad, gz, gy, dface, dcell, dline, dline_y = take(7)

    build_lines(scal, q, zlo, zhi, ylo, yhi, xin, uz, uy, ux)
    wants = mode != "back"
    lap = smooth if wants else None
    for name, u, tend in (("z", uz, "tz"), ("y", uy, "ty")):
        cell_loop(name, u, plus, minus, lap, CELLS)
        spread_rows(name, plus, minus, diffs, base)
        if wants:
            lap_rows(name, smooth, tend_z if name == "z" else tend_y)
    cell_loop("x", ux, plus, minus, lap, ROWS)
    spread_lanes(plus, minus, diffs, base)
    if wants:
        tend_x[0] = jnp.zeros((ROWS, LANES), jnp.float32)
        for c in range(4):
            s = smooth[c, 0:ROWS]
            coef = 0.02 if c < 3 else 0.03
            tend_x[c + 1] = coef * (roll(s, 1) - 2.0 * s + roll(s, -1))

    if mode == "both":
        for c in range(5):
            grad[c] = consts["scale"] * prev[c]
    if mode == "back":
        gather_grad(
            prev, consts["coef"], consts["scale"], own_in, gzlo, gzhi, gylo, gyhi, gxin, total, grad
        )
    if mode != "fwd":
        grad_faces(grad, gz, gy, dface)

    def body(i, carry):
        at = pl.ds(pl.multiple_of(i * 8, 8), 8)
        d = [[diffs[k, c, at, :] for c in range(5)] for k in range(4)]
        g = None if mode == "fwd" else [dface[c, at, :] for c in range(5)]
        value, cells = weno_unit(d, scal, g, wants)
        if wants:
            for c in range(5):
                corr[c, at, :] = value[c]
        if cells is not None:
            for k in range(5):
                for c in range(5):
                    dcell[k, c, at, :] = cells[k][c]
        return carry

    lax.fori_loop(0, FACES // 8, body, 0)

    if wants:
        inside = lane_mask(OWN, 3, 125)
        for c in range(5):
            fz = base[c, 0:104] + corr[c, 0:104] + corr[c, 104:208]
            base[c, 0:104] = fz
            fy = base[c, 104:208] + corr[c, 208:312] + corr[c, 312:416]
            base[c, 104:208] = fy
            fx = base[c, 208:304] + corr[c, 416:512] + corr[c, 512:608]
            tend_z[c, 0:OWN] = tend_z[c, 0:OWN] + base[c, 0:OWN] - base[c, 10 : 10 + OWN]
            tend_y[c, 0:OWN] = tend_y[c, 0:OWN] + base[c, 104 : 104 + OWN] - base[c, 113 : 113 + OWN]
            tend_x[c] = tend_x[c] + roll(fx, 3) - roll(fx, 2)
            for z in range(CZ):
                low = z * CY
                tend_z[c, low : low + CY] = (
                    tend_z[c, low : low + CY] + tend_y[c, pl.ds(z, CY, stride=CZ), :]
                )
            t = (tend_z[c, 0:OWN] + tend_x[c, 0:OWN]) * (inside * DT)
            state_out[c, 0:OWN] = (
                consts["first"] * first[c, 0:OWN] + consts["last"] * (q[c, 0:OWN] + t)
            )
            state_out[c, OWN:ROWS] = jnp.ones((ROWS - OWN, LANES), jnp.float32)
            if mode == "fwd":
                szlo[c, 0:30] = state_out[c, 0:30]
                szhi[c, 0:30] = state_out[c, 60:90]
                for z in range(CZ):
                    low = z * CY
                    sylo[c, pl.ds(z, 3, stride=CZ), :] = state_out[c, low : low + 3]
                    syhi[c, pl.ds(z, 3, stride=CZ), :] = state_out[c, low + 7 : low + 10]

    if mode != "fwd":
        pull_rows("z", dcell, plus, minus, gz, uz, dline)
        for c in range(5):
            own_out[c, 0:OWN] = dline[c, 30:120]
            own_out[c, OWN:ROWS] = jnp.zeros((ROWS - OWN, LANES), jnp.float32)
            dzlo[c, 0:30] = dline[c, 0:30]
            dzhi[c, 0:30] = dline[c, 120:150]
        pull_rows("y", dcell, plus, minus, gy, uy, dline_y)
        for c in range(5):
            flip = -1.0 if c == 2 else 1.0
            dylo[c, 0:27] = dline_y[c, 0:27]
            dyhi[c, 0:27] = dline_y[c, 117:144]
            for g in range(3):
                low = dline_y[c, g * 9 : g * 9 + 9]
                high = dline_y[c, (13 + g) * 9 : (14 + g) * 9]
                at = (5 - g) * 9
                dline_y[c, at : at + 9] = dline_y[c, at : at + 9] + scal[0] * flip * low
                dline_y[c, 27:36] = dline_y[c, 27:36] + scal[1] * low
                at = (12 - g) * 9
                dline_y[c, at : at + 9] = dline_y[c, at : at + 9] + scal[3] * flip * high
                dline_y[c, 108:117] = dline_y[c, 108:117] + scal[4] * high
            for z in range(CZ):
                low = z * CY
                own_out[c, low : low + CY] = (
                    own_out[c, low : low + CY] + dline_y[c, pl.ds(27 + z, CY, stride=CZ), :]
                )
        pull_lanes(dcell, plus, minus, grad, ux, dline)
        rows_on = jnp.where(
            lax.broadcasted_iota(jnp.int32, (ROWS, LANES), 0) < OWN, 1.0, 0.0
        ).astype(jnp.float32)
        for c in range(5):
            flip = -1.0 if c == 1 else 1.0
            v = dline[c, 0:ROWS] * rows_on
            dx[c] = v * (
                lane_mask(ROWS, 0, 3) * scal[8] + lane_mask(ROWS, 125, 128) * scal[11]
            )
            acc = v + own_out[c]
            for g in range(3):
                low = v * lane_mask(ROWS, g, g + 1)
                high = v * lane_mask(ROWS, 125 + g, 126 + g)
                acc = acc + scal[6] * flip * roll(low, 5 - 2 * g) + scal[7] * roll(low, 3 - g)
                acc = acc + scal[9] * flip * roll(high, -1 - 2 * g) + scal[10] * roll(high, -1 - g)
            own_out[c] = acc * lane_mask(ROWS, 3, 125)


def finish_kernel(coef, prev, own, zlo, zhi, ylo, yhi, xin, total):
    gather_grad(prev, coef, None, own, zlo, zhi, ylo, yhi, xin, total, None)


FULL = (5, ROWS, LANES)
EDGE = (5, 32, LANES)


def shape(dims):
    return jax.ShapeDtypeStruct(dims, jnp.float32)


def vmem(dims):
    return pltpu.VMEM(dims, jnp.float32)


def section(mode, consts, *args):
    outs = []
    if mode != "back":
        outs.append(FULL)
    if mode == "fwd":
        outs += [EDGE] * 4
    if mode == "back":
        outs.append(FULL)
    if mode != "fwd":
        outs += [FULL] + [EDGE] * 4 + [FULL]
    line = (5, CELLS, LANES)
    scratch = [line, line, FULL, line, line, (4, CELLS, LANES), (4, 5, FACES, LANES)]
    if mode != "back":
        scratch += [(5, 304, LANES), FULL, FULL, FULL, (5, FACES, LANES)]
    if mode != "fwd":
        gpad = (5, GPAD, LANES)
        scratch += [FULL, gpad, gpad, (5, FACES, LANES), (5, 5, FACES, LANES), line, line]
    return pl.pallas_call(
        functools.partial(section_kernel, mode, consts),
        out_shape=[shape(s) for s in outs],
        in_specs=[pl.BlockSpec(memory_space=pltpu.SMEM)]
        + [pl.BlockSpec(memory_space=pltpu.VMEM)] * (len(args) - 1),
        out_specs=[pl.BlockSpec(memory_space=pltpu.VMEM)] * len(outs),
        scratch_shapes=[vmem(s) for s in scratch],
        compiler_params=pltpu.CompilerParams(vmem_limit_bytes=48 * 1024 * 1024),
        name="section_" + mode,
    )(*args)


def flat(field, fill):
    lanes = jnp.pad(
        field, ((0, 0), (0, 0), (0, 0), (3, 3)), constant_values=fill
    ).reshape(5, OWN, LANES)
    return jnp.pad(lanes, ((0, 0), (0, ROWS - OWN), (0, 0)), constant_values=fill)


def unflat(field):
    return field[:, :OWN].reshape(5, CZ, CY, LANES)[..., 3 : 3 + CX]


def swap(down, up, axis, periodic):
    count = lax.axis_size(axis)
    forward = [(i, i + 1) for i in range(count - 1)]
    if periodic:
        forward.append((count - 1, 0))
    backward = [(t, s) for s, t in forward]
    return lax.ppermute(up, axis, forward), lax.ppermute(down, axis, backward)


def exchange(full, zlo, zhi, ylo, yhi):
    from_z = swap(zlo, zhi, "gz", True)
    from_y = swap(ylo, yhi, "gy", False)
    partner = lax.ppermute(full, "gx", [(0, 1), (1, 0)])
    return (*from_z, *from_y, partner)


def on_device(density, momentum, energy, cotangent, bc_codes, weight_in, weight_out):
    state = flat(jnp.concatenate([density[None], momentum, energy[None]], 0), 1.0)
    cot = flat(cotangent, 0.0)
    y_place = lax.axis_index("gy")
    x_place = lax.axis_index("gx")
    edges = jnp.stack(
        [
            y_place == 0,
            y_place == lax.axis_size("gy") - 1,
            x_place == 0,
            x_place == lax.axis_size("gx") - 1,
        ]
    ).astype(jnp.float32)
    wall = (bc_codes == 0).astype(jnp.float32)
    sides = jnp.stack([edges * wall, edges * (1.0 - wall), 1.0 - edges], 1).reshape(12)
    scal = jnp.concatenate([sides, weight_in.reshape(-1), weight_out.reshape(-1)])

    rows = state[:, :OWN].reshape(5, CZ, CY, LANES)
    tail = lambda v, n: jnp.pad(v.reshape(5, n, LANES), ((0, 0), (0, 32 - n), (0, 0)))
    by_y = jnp.swapaxes(rows, 1, 2)
    halo_one = exchange(
        state,
        tail(rows[:, 0:3], 30),
        tail(rows[:, -3:], 30),
        tail(by_y[:, 0:3], 27),
        tail(by_y[:, -3:], 27),
    )
    one, *edge = section("fwd", dict(first=0.0, last=1.0), scal, state, *halo_one, state)
    halo_two = exchange(one, *edge)
    two, *edge = section("fwd", dict(first=0.75, last=0.25), scal, one, *halo_two, state)
    halo_three = exchange(two, *edge)
    new_state, own, *edge, dx = section(
        "both",
        dict(first=1.0 / 3.0, last=2.0 / 3.0, scale=DT * 2.0 / 3.0),
        scal,
        two,
        *halo_three,
        state,
        cot,
    )
    back = exchange(dx, *edge)
    grad_two, own, *edge, dx = section(
        "back", dict(coef=2.0 / 3.0, scale=0.25 * DT), scal, one, *halo_two, cot, own, *back
    )
    back = exchange(dx, *edge)
    grad_one, own, *edge, dx = section(
        "back", dict(coef=0.25, scale=DT), scal, state, *halo_one, grad_two, own, *back
    )
    back = exchange(dx, *edge)
    total = pl.pallas_call(
        functools.partial(finish_kernel, 1.0),
        out_shape=shape(FULL),
        name="finish",
    )(grad_one, own, *back)
    total = total + 0.75 * grad_two + (1.0 / 3.0) * cot
    return (unflat(new_state), unflat(total))


def solution(mesh):
    in_specs = (
        P(("groups", "gz"), "gy", "gx"),
        P(None, ("groups", "gz"), "gy", "gx"),
        P(("groups", "gz"), "gy", "gx"),
        P(None, ("groups", "gz"), "gy", "gx"),
        P("groups"),
        P(),
        P(),
    )
    out_specs = (P(None, ("groups", "gz"), "gy", "gx"), P(None, ("groups", "gz"), "gy", "gx"))
    return jax.shard_map(
        on_device, mesh=mesh, in_specs=in_specs, out_specs=out_specs, check_vma=False
    )
```

```python
import functools
import jax
import jax.numpy as jnp
from jax import lax
from jax.experimental import pallas as pl
from jax.experimental.pallas import tpu as pltpu
from jax.sharding import PartitionSpec as P

DT = 0.06
HID = 16
CZ, CY, CX = 9, 10, 122
ROWS = 96
LANES = 128
OWN = CZ * CY
FACE_ROWS = {"z": (0, 104, 104), "y": (208, 312, 104), "x": (416, 512, 96)}
FACES = 608
CELLS = 160
GPAD = 208
PITCH = {"z": 10, "y": 9}
COMP = {"z": 3, "y": 2, "x": 1}
W_IN = 12
W_OUT = 12 + 3 * HID


def roll(v, amount):
    return pltpu.roll(v, amount % LANES, 1)


def lane_mask(rows, low, high):
    lanes = lax.broadcasted_iota(jnp.int32, (rows, LANES), 1)
    return jnp.where((lanes >= low) & (lanes < high), 1.0, 0.0).astype(jnp.float32)


def cell_terms(comp, u):
    inverse = 1.0 / u[0]
    veloc = [u[i] * inverse for i in (1, 2, 3)]
    press = 0.4 * (u[4] - 0.5 * (u[1] * veloc[0] + u[2] * veloc[1] + u[3] * veloc[2]))
    normal = veloc[comp - 1]
    flux = [u[comp]]
    for i in (1, 2, 3):
        term = u[i] * normal
        flux.append(term + press if i == comp else term)
    flux.append((u[4] + press) * normal)
    return flux, veloc + [press * inverse]


def weno_unit(d, scal, grad, want_value):
    ratios, inverses = [], []
    feats = [0.0, 0.0, 0.0]
    for c in range(5):
        d1, d2, d3, d4 = d[0][c], d[1][c], d[2][c], d[3][c]
        b0 = 4.0 * d1 * d1 + d2 * (10.0 * d2 - 11.0 * d1)
        b1 = 4.0 * d3 * d3 + d2 * (4.0 * d2 - 5.0 * d3)
        b2 = 4.0 * d4 * d4 + d3 * (10.0 * d3 - 11.0 * d4)
        inv = 1.0 / (b0 + b1 + b2 + 0.3)
        r = [b0 * inv, b1 * inv, b2 * inv]
        ratios.append(r)
        inverses.append(inv)
        feats = [feats[k] + r[k] for k in range(3)]
    feats = [0.2 * f for f in feats]
    hidden = []
    for j in range(HID):
        pre = scal[W_IN + j] * feats[0]
        pre = pre + scal[W_IN + HID + j] * feats[1]
        pre = pre + scal[W_IN + 2 * HID + j] * feats[2]
        hidden.append(jnp.tanh(pre))
    linear = (0.1, 0.6, 0.3)
    gates, slopes = [], []
    for k in range(3):
        s = scal[W_OUT + k] * hidden[0]
        for j in range(1, HID):
            s = s + scal[W_OUT + 3 * j + k] * hidden[j]
        e = jnp.exp(-jnp.abs(s))
        gates.append(linear[k] * (jnp.maximum(s, 0.0) + jnp.log(1.0 + e) + 0.05))
        if grad is not None:
            slopes.append(linear[k] * jnp.where(s >= 0.0, 1.0, e) / (1.0 + e))
    inv_sum = 1.0 / (gates[0] + gates[1] + gates[2])
    w = [g * inv_sum for g in gates]
    a = [
        w[0] * (-1.0 / 3.0),
        (5.0 * w[0] + w[1]) * (1.0 / 6.0),
        (w[1] + 2.0 * w[2]) * (1.0 / 3.0),
        w[2] * (-1.0 / 6.0),
    ]
    value = None
    if want_value:
        value = [
            a[0] * d[0][c] + a[1] * d[1][c] + a[2] * d[2][c] + a[3] * d[3][c] for c in range(5)
        ]
    if grad is None:
        return value, None
    q = []
    for i in range(4):
        t = grad[0] * d[i][0]
        for c in range(1, 5):
            t = t + grad[c] * d[i][c]
        q.append(t * (1.0 / 6.0))
    dw = [5.0 * q[1] - 2.0 * q[0], q[1] + 2.0 * q[2], 4.0 * q[2] - q[3]]
    mid = w[0] * dw[0] + w[1] * dw[1] + w[2] * dw[2]
    ds = [(dw[k] - mid) * inv_sum * slopes[k] for k in range(3)]
    e = [0.0, 0.0, 0.0]
    for j in range(HID):
        dh = scal[W_OUT + 3 * j] * ds[0]
        dh = dh + scal[W_OUT + 3 * j + 1] * ds[1]
        dh = dh + scal[W_OUT + 3 * j + 2] * ds[2]
        dpre = dh * (1.0 - hidden[j] * hidden[j])
        e = [e[k] + scal[W_IN + HID * k + j] * dpre for k in range(3)]
    e = [0.2 * v for v in e]
    cells = [[], [], [], [], []]
    for c in range(5):
        d1, d2, d3, d4 = d[0][c], d[1][c], d[2][c], d[3][c]
        r, inv, gc = ratios[c], inverses[c], grad[c]
        m = e[0] * r[0] + e[1] * r[1] + e[2] * r[2]
        g0, g1, g2 = (e[0] - m) * inv, (e[1] - m) * inv, (e[2] - m) * inv
        dd1 = a[0] * gc + g0 * (8.0 * d1 - 11.0 * d2)
        dd2 = a[1] * gc + g0 * (20.0 * d2 - 11.0 * d1) + g1 * (8.0 * d2 - 5.0 * d3)
        dd3 = a[2] * gc + g1 * (8.0 * d3 - 5.0 * d2) + g2 * (20.0 * d3 - 11.0 * d4)
        dd4 = a[3] * gc + g2 * (8.0 * d4 - 11.0 * d3)
        cells[0].append(-dd1)
        cells[1].append(dd1 - dd2)
        cells[2].append(dd2 - dd3 + gc)
        cells[3].append(dd3 - dd4)
        cells[4].append(dd4)
    return value, cells


def build_lines(scal, q, zlo, zhi, ylo, yhi, xin, uz, uy, ux):
    for c in range(5):
        uz[c, 0:30] = zlo[c, 0:30]
        uz[c, 30:120] = q[c, 0:OWN]
        uz[c, 120:150] = zhi[c, 0:30]
        uz[c, 150:160] = jnp.ones((10, LANES), jnp.float32)
        for z in range(CZ):
            uy[c, pl.ds(27 + z, CY, stride=CZ), :] = q[c, z * CY : (z + 1) * CY]
        flip = -1.0 if c == 2 else 1.0
        for g in range(3):
            low = scal[0] * flip * uy[c, (5 - g) * 9 : (6 - g) * 9] + scal[1] * uy[c, 27:36]
            uy[c, g * 9 : g * 9 + 9] = low + scal[2] * ylo[c, g * 9 : g * 9 + 9]
            high = scal[3] * flip * uy[c, (12 - g) * 9 : (13 - g) * 9] + scal[4] * uy[c, 108:117]
            uy[c, (13 + g) * 9 : (14 + g) * 9] = high + scal[5] * yhi[c, g * 9 : g * 9 + 9]
        uy[c, 144:160] = jnp.ones((16, LANES), jnp.float32)
        flip = -1.0 if c == 1 else 1.0
        own = q[c]
        partner = xin[c]
        value = own * lane_mask(ROWS, 3, 125)
        low = scal[8] * roll(partner, 6)
        high = scal[11] * roll(partner, 122)
        value = value + lane_mask(ROWS, 0, 3) * low + lane_mask(ROWS, 125, 128) * high
        for g in range(3):
            at_low = lane_mask(ROWS, g, g + 1)
            value = value + at_low * (
                scal[6] * flip * roll(own, -(5 - 2 * g)) + scal[7] * roll(own, g - 3)
            )
            at_high = lane_mask(ROWS, 125 + g, 126 + g)
            value = value + at_high * (
                scal[9] * flip * roll(own, 1 + 2 * g) + scal[10] * roll(own, 1 + g)
            )
        ux[c] = value


def cell_loop(name, u, plus, minus, smooth, rows):
    def body(i, carry):
        at = pl.ds(pl.multiple_of(i * 8, 8), 8)
        cells = [u[c, at, :] for c in range(5)]
        flux, sv = cell_terms(COMP[name], cells)
        for c in range(5):
            plus[c, at, :] = 0.5 * flux[c] + cells[c]
            minus[c, at, :] = 0.5 * flux[c] - cells[c]
        if smooth is not None:
            for c in range(4):
                smooth[c, at, :] = sv[c]
        return carry

    lax.fori_loop(0, rows // 8, body, 0)


def spread_rows(name, plus, minus, diffs, base):
    p = PITCH[name]
    at_plus, at_minus, count = FACE_ROWS[name]
    for c in range(5):
        for start, size in ((0, 56), (56, 48)):
            f = [plus[c, start + k * p : start + k * p + size] for k in range(5)]
            for i in range(4):
                diffs[i, c, at_plus + start : at_plus + start + size] = f[i + 1] - f[i]
            middle = f[2]
            f = [minus[c, start + k * p : start + k * p + size] for k in range(1, 6)]
            for i in range(4):
                diffs[i, c, at_minus + start : at_minus + start + size] = f[3 - i] - f[4 - i]
            if base is not None:
                base[c, at_plus // 2 + start : at_plus // 2 + start + size] = middle + f[2]


def spread_lanes(plus, minus, diffs, base):
    at_plus, at_minus, count = FACE_ROWS["x"]
    for c in range(5):
        for start in (0, 48):
            v = plus[c, start : start + 48]
            diff = roll(v, -1) - v
            for i in range(4):
                diffs[i, c, at_plus + start : at_plus + start + 48] = roll(diff, -i)
            m = minus[c, start : start + 48]
            diff = m - roll(m, -1)
            for i in range(4):
                diffs[i, c, at_minus + start : at_minus + start + 48] = roll(diff, i - 4)
            if base is not None:
                base[c, at_plus // 2 + start : at_plus // 2 + start + 48] = roll(v, -2) + roll(
                    m, -3
                )


def lap_rows(name, smooth, out):
    p = PITCH[name]
    out[0] = jnp.zeros((ROWS, LANES), jnp.float32)
    for c in range(4):
        coef = 0.02 if c < 3 else 0.03
        s = [smooth[c, k * p : k * p + OWN] for k in (2, 3, 4)]
        out[c + 1, 0:OWN] = coef * (s[2] - 2.0 * s[1] + s[0])


def gather_grad(prev, coef, scale, own, zlo, zhi, ylo, yhi, xin, total, grad):
    for c in range(5):
        x = lane_mask(ROWS, 122, 125) * roll(xin[c], 122) + lane_mask(ROWS, 3, 6) * roll(xin[c], 6)
        total[c] = coef * prev[c] + own[c] + x
        total[c, 0:30] = total[c, 0:30] + zlo[c, 0:30]
        total[c, 60:90] = total[c, 60:90] + zhi[c, 0:30]
        for z in range(CZ):
            low = z * CY
            total[c, low : low + 3] = total[c, low : low + 3] + ylo[c, pl.ds(z, 3, stride=CZ), :]
            total[c, low + 7 : low + 10] = (
                total[c, low + 7 : low + 10] + yhi[c, pl.ds(z, 3, stride=CZ), :]
            )
        if grad is not None:
            grad[c] = scale * total[c]


def grad_faces(grad, gz, gy, dface):
    for c in range(5):
        gz[c] = jnp.zeros((GPAD, LANES), jnp.float32)
        gy[c] = jnp.zeros((GPAD, LANES), jnp.float32)
        gz[c, 40 : 40 + OWN] = grad[c, 0:OWN]
        for z in range(CZ):
            gy[c, pl.ds(36 + z, CY, stride=CZ), :] = grad[c, z * CY : (z + 1) * CY]
        dz = gz[c, 40:144] - gz[c, 30:134]
        dy = gy[c, 36:140] - gy[c, 27:131]
        g = grad[c]
        dx = roll(g, -3) - roll(g, -2)
        dface[c, 0:104] = dz
        dface[c, 104:208] = dz
        dface[c, 208:312] = dy
        dface[c, 312:416] = dy
        dface[c, 416:512] = dx
        dface[c, 512:608] = dx


def pull_rows(name, dcell, plus, minus, gpad, u, out):
    p = PITCH[name]
    at_plus, at_minus, count = FACE_ROWS[name]
    for c in range(5):
        plus[c] = jnp.zeros((CELLS, LANES), jnp.float32)
        minus[c] = jnp.zeros((CELLS, LANES), jnp.float32)
        for k in range(5):
            low = k * p
            plus[c, low : low + 104] = (
                plus[c, low : low + 104] + dcell[k, c, at_plus : at_plus + 104]
            )
            low = (5 - k) * p
            minus[c, low : low + 104] = (
                minus[c, low : low + 104] + dcell[k, c, at_minus : at_minus + 104]
            )
        if c > 0:
            coef = 0.02 if c < 4 else 0.03
            g = [gpad[c, k * p : k * p + CELLS] for k in range(3)]
            out[c] = coef * (g[0] - 2.0 * g[1] + g[2])
    pull_cells(name, plus, minus, u, out, CELLS)


def pull_lanes(dcell, plus, minus, grad, u, out):
    at_plus, at_minus, count = FACE_ROWS["x"]
    for c in range(5):
        sp = dcell[0, c, at_plus : at_plus + ROWS]
        sm = roll(dcell[0, c, at_minus : at_minus + ROWS], 5)
        for k in range(1, 5):
            sp = sp + roll(dcell[k, c, at_plus : at_plus + ROWS], k)
            sm = sm + roll(dcell[k, c, at_minus : at_minus + ROWS], 5 - k)
        plus[c, 0:ROWS] = sp
        minus[c, 0:ROWS] = sm
        if c > 0:
            coef = 0.02 if c < 4 else 0.03
            g = grad[c]
            out[c, 0:ROWS] = coef * (roll(g, 1) - 2.0 * g + roll(g, -1))
    pull_cells("x", plus, minus, u, out, ROWS)


def pull_cells(name, plus, minus, u, out, rows):
    def body(i, carry):
        at = pl.ds(pl.multiple_of(i * 8, 8), 8)
        cells = [u[c, at, :] for c in range(5)]
        dp = [plus[c, at, :] for c in range(5)]
        dm = [minus[c, at, :] for c in range(5)]
        dsv = [out[c, at, :] for c in range(1, 5)]
        unused, back = jax.vjp(functools.partial(cell_terms, COMP[name]), cells)
        (du,) = back(([0.5 * (dp[c] + dm[c]) for c in range(5)], dsv))
        for c in range(5):
            out[c, at, :] = du[c] + dp[c] - dm[c]
        return carry

    lax.fori_loop(0, rows // 8, body, 0)


def section(mode, consts, scal, q, halo, first, prev, own_in, halo_grad, state_out, sends, total,
            own_out, grad_sends, dx, work):
    zlo, zhi, ylo, yhi, xin = halo
    uz, uy, ux, plus, minus, smooth, diffs, base, tend_z, tend_y, tend_x, corr = work[:12]
    grad, gz, gy, dface, dcell, dline, dline_y = work[12:]
    if mode == "back":
        base = None
    if mode != "fwd":
        dzlo, dzhi, dylo, dyhi = grad_sends

    build_lines(scal, q, zlo, zhi, ylo, yhi, xin, uz, uy, ux)
    wants = mode != "back"
    lap = smooth if wants else None
    for name, u, tend in (("z", uz, "tz"), ("y", uy, "ty")):
        cell_loop(name, u, plus, minus, lap, CELLS)
        spread_rows(name, plus, minus, diffs, base)
        if wants:
            lap_rows(name, smooth, tend_z if name == "z" else tend_y)
    cell_loop("x", ux, plus, minus, lap, ROWS)
    spread_lanes(plus, minus, diffs, base)
    if wants:
        tend_x[0] = jnp.zeros((ROWS, LANES), jnp.float32)
        for c in range(4):
            s = smooth[c, 0:ROWS]
            coef = 0.02 if c < 3 else 0.03
            tend_x[c + 1] = coef * (roll(s, 1) - 2.0 * s + roll(s, -1))

    if mode == "both":
        for c in range(5):
            grad[c] = consts["scale"] * prev[c]
    if mode == "back":
        gather_grad(prev, consts["coef"], consts["scale"], own_in, *halo_grad(), total, grad)
    if mode != "fwd":
        grad_faces(grad, gz, gy, dface)

    def body(i, carry):
        at = pl.ds(pl.multiple_of(i * 8, 8), 8)
        d = [[diffs[k, c, at, :] for c in range(5)] for k in range(4)]
        g = None if mode == "fwd" else [dface[c, at, :] for c in range(5)]
        value, cells = weno_unit(d, scal, g, wants)
        if wants:
            for c in range(5):
                corr[c, at, :] = value[c]
        if cells is not None:
            for k in range(5):
                for c in range(5):
                    dcell[k, c, at, :] = cells[k][c]
        return carry

    lax.fori_loop(0, FACES // 8, body, 0)

    if wants:
        inside = lane_mask(OWN, 3, 125)
        for c in range(5):
            fz = base[c, 0:104] + corr[c, 0:104] + corr[c, 104:208]
            base[c, 0:104] = fz
            fy = base[c, 104:208] + corr[c, 208:312] + corr[c, 312:416]
            base[c, 104:208] = fy
            fx = base[c, 208:304] + corr[c, 416:512] + corr[c, 512:608]
            tend_z[c, 0:OWN] = tend_z[c, 0:OWN] + base[c, 0:OWN] - base[c, 10 : 10 + OWN]
            tend_y[c, 0:OWN] = tend_y[c, 0:OWN] + base[c, 104 : 104 + OWN] - base[c, 113 : 113 + OWN]
            tend_x[c] = tend_x[c] + roll(fx, 3) - roll(fx, 2)
            for z in range(CZ):
                low = z * CY
                tend_z[c, low : low + CY] = (
                    tend_z[c, low : low + CY] + tend_y[c, pl.ds(z, CY, stride=CZ), :]
                )
            t = (tend_z[c, 0:OWN] + tend_x[c, 0:OWN]) * (inside * DT)
            state_out[c, 0:OWN] = (
                consts["first"] * first[c, 0:OWN] + consts["last"] * (q[c, 0:OWN] + t)
            )
            state_out[c, OWN:ROWS] = jnp.ones((ROWS - OWN, LANES), jnp.float32)
        if mode == "fwd":
            cut_edges(state_out, sends)

    if mode != "fwd":
        pull_rows("z", dcell, plus, minus, gz, uz, dline)
        for c in range(5):
            own_out[c, 0:OWN] = dline[c, 30:120]
            own_out[c, OWN:ROWS] = jnp.zeros((ROWS - OWN, LANES), jnp.float32)
            dzlo[c, 0:30] = dline[c, 0:30]
            dzhi[c, 0:30] = dline[c, 120:150]
        pull_rows("y", dcell, plus, minus, gy, uy, dline_y)
        for c in range(5):
            flip = -1.0 if c == 2 else 1.0
            dylo[c, 0:27] = scal[2] * dline_y[c, 0:27]
            dyhi[c, 0:27] = scal[5] * dline_y[c, 117:144]
            for g in range(3):
                low = dline_y[c, g * 9 : g * 9 + 9]
                high = dline_y[c, (13 + g) * 9 : (14 + g) * 9]
                at = (5 - g) * 9
                dline_y[c, at : at + 9] = dline_y[c, at : at + 9] + scal[0] * flip * low
                dline_y[c, 27:36] = dline_y[c, 27:36] + scal[1] * low
                at = (12 - g) * 9
                dline_y[c, at : at + 9] = dline_y[c, at : at + 9] + scal[3] * flip * high
                dline_y[c, 108:117] = dline_y[c, 108:117] + scal[4] * high
            for z in range(CZ):
                low = z * CY
                own_out[c, low : low + CY] = (
                    own_out[c, low : low + CY] + dline_y[c, pl.ds(27 + z, CY, stride=CZ), :]
                )
        pull_lanes(dcell, plus, minus, grad, ux, dline)
        rows_on = jnp.where(
            lax.broadcasted_iota(jnp.int32, (ROWS, LANES), 0) < OWN, 1.0, 0.0
        ).astype(jnp.float32)
        for c in range(5):
            flip = -1.0 if c == 1 else 1.0
            v = dline[c, 0:ROWS] * rows_on
            dx[c] = v * (
                lane_mask(ROWS, 0, 3) * scal[8] + lane_mask(ROWS, 125, 128) * scal[11]
            )
            acc = v + own_out[c]
            for g in range(3):
                low = v * lane_mask(ROWS, g, g + 1)
                high = v * lane_mask(ROWS, 125 + g, 126 + g)
                acc = acc + scal[6] * flip * roll(low, 5 - 2 * g) + scal[7] * roll(low, 3 - g)
                acc = acc + scal[9] * flip * roll(high, -1 - 2 * g) + scal[10] * roll(high, -1 - g)
            own_out[c] = acc * lane_mask(ROWS, 3, 125)


FULL = (5, ROWS, LANES)
EDGE = (5, 32, LANES)
LINE = (5, CELLS, LANES)
GLINE = (5, GPAD, LANES)
WORK = [LINE, LINE, FULL, LINE, LINE, (4, CELLS, LANES), (4, 5, FACES, LANES)]
WORK += [(5, 304, LANES), FULL, FULL, FULL, (5, FACES, LANES)]
WORK += [FULL, GLINE, GLINE, (5, FACES, LANES), (5, 5, FACES, LANES), LINE, LINE]


def cut_edges(field, sends):
    szlo, szhi, sylo, syhi = sends
    for c in range(5):
        szlo[c, 0:30] = field[c, 0:30]
        szhi[c, 0:30] = field[c, 60:90]
        for z in range(CZ):
            low = z * CY
            sylo[c, pl.ds(z, 3, stride=CZ), :] = field[c, low : low + 3]
            syhi[c, pl.ds(z, 3, stride=CZ), :] = field[c, low + 7 : low + 10]


def step_kernel(sizes, scal, state, cot, new_out, grad_out, one, two, grad_two, grad_one, own, dx,
                sends, takes, xtakes, send_sem, recv_sem, *work):
    peers = []
    for axis in ("gz", "gy"):
        place, count = lax.axis_index(axis), sizes[axis]
        peers.append({axis: lax.rem(place + count - 1, count)})
        peers.append({axis: lax.rem(place + 1, count)})
    peers.append({"gx": 1 - lax.axis_index("gx")})
    mesh_id = pl.DeviceIdType.MESH

    barrier = pltpu.get_barrier_semaphore()
    for peer in peers:
        pl.semaphore_signal(barrier, inc=1, device_id=peer, device_id_type=mesh_id)
    pl.semaphore_wait(barrier, len(peers))

    flights = {}

    def send_to(turn, full):
        flights[turn] = []
        for i, peer in enumerate(peers):
            copy = pltpu.make_async_remote_copy(
                src_ref=full if i == 4 else sends.at[turn, i],
                dst_ref=xtakes.at[turn] if i == 4 else takes.at[turn, i ^ 1],
                send_sem=send_sem.at[turn, i],
                recv_sem=recv_sem.at[turn, i],
                device_id=peer,
                device_id_type=mesh_id,
            )
            copy.start()
            flights[turn].append(copy)

    def arrive(turn):
        for copy in flights[turn]:
            copy.wait_recv()
        return halo(turn)

    def halo(turn):
        return [takes.at[turn, i] for i in range(4)] + [xtakes.at[turn]]

    def edges(turn):
        return [sends.at[turn, i] for i in range(4)]

    cut_edges(state, edges(0))
    send_to(0, state)
    section("fwd", dict(first=0.0, last=1.0), scal, state, arrive(0), state, None, None, None,
            one, edges(1), None, None, None, None, work)
    send_to(1, one)
    section("fwd", dict(first=0.75, last=0.25), scal, one, arrive(1), state, None, None, None,
            two, edges(2), None, None, None, None, work)
    send_to(2, two)
    section("both", dict(first=1.0 / 3.0, last=2.0 / 3.0, scale=DT * 2.0 / 3.0), scal, two,
            arrive(2), state, cot, None, None, new_out, None, None, own, edges(3), dx.at[0], work)
    send_to(3, dx.at[0])
    section("back", dict(coef=2.0 / 3.0, scale=0.25 * DT), scal, one, halo(1), None, cot, own,
            lambda: arrive(3), None, None, grad_two, own, edges(4), dx.at[1], work)
    send_to(4, dx.at[1])
    section("back", dict(coef=0.25, scale=DT), scal, state, halo(0), None, grad_two, own,
            lambda: arrive(4), None, None, grad_one, own, edges(5), dx.at[2], work)
    send_to(5, dx.at[2])
    for c in range(5):
        grad_one[c] = grad_one[c] + 0.75 * grad_two[c] + (1.0 / 3.0) * cot[c]
    gather_grad(grad_one, 1.0, None, own, *arrive(5), grad_out, None)
    for turn in range(6):
        for copy in flights[turn]:
            copy.wait_send()


def flat(field, fill):
    lanes = jnp.pad(
        field, ((0, 0), (0, 0), (0, 0), (3, 3)), constant_values=fill
    ).reshape(5, OWN, LANES)
    return jnp.pad(lanes, ((0, 0), (0, ROWS - OWN), (0, 0)), constant_values=fill)


def unflat(field):
    return field[:, :OWN].reshape(5, CZ, CY, LANES)[..., 3 : 3 + CX]


def run_step(scal, state, cot):
    shape = jax.ShapeDtypeStruct(FULL, jnp.float32)
    vmem = pl.BlockSpec(memory_space=pltpu.VMEM)
    scratch = [FULL] * 5 + [(3,) + FULL, (6, 4) + EDGE, (6, 4) + EDGE, (6,) + FULL]
    sizes = {axis: lax.axis_size(axis) for axis in ("gz", "gy")}
    return pl.pallas_call(
        functools.partial(step_kernel, sizes),
        out_shape=[shape, shape],
        in_specs=[pl.BlockSpec(memory_space=pltpu.SMEM), vmem, vmem],
        out_specs=[vmem, vmem],
        scratch_shapes=[pltpu.VMEM(s, jnp.float32) for s in scratch]
        + [pltpu.SemaphoreType.DMA((6, 5))] * 2
        + [pltpu.VMEM(s, jnp.float32) for s in WORK],
        compiler_params=pltpu.CompilerParams(
            vmem_limit_bytes=56 * 1024 * 1024, collective_id=0, has_side_effects=True
        ),
        name="step",
    )(scal, state, cot)


def on_device(density, momentum, energy, cotangent, bc_codes, weight_in, weight_out):
    state = flat(jnp.concatenate([density[None], momentum, energy[None]], 0), 1.0)
    cot = flat(cotangent, 0.0)
    y_place = lax.axis_index("gy")
    x_place = lax.axis_index("gx")
    edges = jnp.stack(
        [
            y_place == 0,
            y_place == lax.axis_size("gy") - 1,
            x_place == 0,
            x_place == lax.axis_size("gx") - 1,
        ]
    ).astype(jnp.float32)
    wall = (bc_codes == 0).astype(jnp.float32)
    sides = jnp.stack([edges * wall, edges * (1.0 - wall), 1.0 - edges], 1).reshape(12)
    scal = jnp.concatenate([sides, weight_in.reshape(-1), weight_out.reshape(-1)])

    new_state, total = run_step(scal, state, cot)
    return (unflat(new_state), unflat(total))


def solution(mesh):
    in_specs = (
        P(("groups", "gz"), "gy", "gx"),
        P(None, ("groups", "gz"), "gy", "gx"),
        P(("groups", "gz"), "gy", "gx"),
        P(None, ("groups", "gz"), "gy", "gx"),
        P("groups"),
        P(),
        P(),
    )
    out_specs = (P(None, ("groups", "gz"), "gy", "gx"), P(None, ("groups", "gz"), "gy", "gx"))
    return jax.shard_map(
        on_device, mesh=mesh, in_specs=in_specs, out_specs=out_specs, check_vma=False
    )
```

```python
import functools
import jax
import jax.numpy as jnp
from jax import lax
from jax.experimental import pallas as pl
from jax.experimental.pallas import tpu as pltpu
from jax.sharding import PartitionSpec as P

DT = 0.06
HID = 16
CZ, CY, CX = 9, 10, 122
ROWS = 96
LANES = 128
OWN = CZ * CY
FACE_ROWS = {"z": (0, 104, 104), "y": (208, 312, 104), "x": (416, 512, 96)}
FACES = 608
CELLS = 160
GPAD = 208
PITCH = {"z": 10, "y": 9}
COMP = {"z": 3, "y": 2, "x": 1}
W_IN = 12
W_OUT = 12 + 3 * HID


def roll(v, amount):
    return pltpu.roll(v, amount % LANES, 1)


def lane_mask(rows, low, high):
    lanes = lax.broadcasted_iota(jnp.int32, (rows, LANES), 1)
    return jnp.where((lanes >= low) & (lanes < high), 1.0, 0.0).astype(jnp.float32)


def cell_terms(comp, u):
    inverse = 1.0 / u[0]
    veloc = [u[i] * inverse for i in (1, 2, 3)]
    press = 0.4 * (u[4] - 0.5 * (u[1] * veloc[0] + u[2] * veloc[1] + u[3] * veloc[2]))
    normal = veloc[comp - 1]
    flux = [u[comp]]
    for i in (1, 2, 3):
        term = u[i] * normal
        flux.append(term + press if i == comp else term)
    flux.append((u[4] + press) * normal)
    return flux, veloc + [press * inverse]


def weno_unit(d, scal, grad, want_value):
    ratios, inverses = [], []
    feats = [0.0, 0.0, 0.0]
    for c in range(5):
        d1, d2, d3, d4 = d[0][c], d[1][c], d[2][c], d[3][c]
        b0 = 4.0 * d1 * d1 + d2 * (10.0 * d2 - 11.0 * d1)
        b1 = 4.0 * d3 * d3 + d2 * (4.0 * d2 - 5.0 * d3)
        b2 = 4.0 * d4 * d4 + d3 * (10.0 * d3 - 11.0 * d4)
        inv = 1.0 / (b0 + b1 + b2 + 0.3)
        r = [b0 * inv, b1 * inv, b2 * inv]
        ratios.append(r)
        inverses.append(inv)
        feats = [feats[k] + r[k] for k in range(3)]
    feats = [0.2 * f for f in feats]
    hidden = []
    for j in range(HID):
        pre = scal[W_IN + j] * feats[0]
        pre = pre + scal[W_IN + HID + j] * feats[1]
        pre = pre + scal[W_IN + 2 * HID + j] * feats[2]
        hidden.append(jnp.tanh(pre))
    linear = (0.1, 0.6, 0.3)
    gates, slopes = [], []
    for k in range(3):
        s = scal[W_OUT + k] * hidden[0]
        for j in range(1, HID):
            s = s + scal[W_OUT + 3 * j + k] * hidden[j]
        e = jnp.exp(-jnp.abs(s))
        gates.append(linear[k] * (jnp.maximum(s, 0.0) + jnp.log(1.0 + e) + 0.05))
        if grad is not None:
            slopes.append(linear[k] * jnp.where(s >= 0.0, 1.0, e) / (1.0 + e))
    inv_sum = 1.0 / (gates[0] + gates[1] + gates[2])
    w = [g * inv_sum for g in gates]
    a = [
        w[0] * (-1.0 / 3.0),
        (5.0 * w[0] + w[1]) * (1.0 / 6.0),
        (w[1] + 2.0 * w[2]) * (1.0 / 3.0),
        w[2] * (-1.0 / 6.0),
    ]
    value = None
    if want_value:
        value = [
            a[0] * d[0][c] + a[1] * d[1][c] + a[2] * d[2][c] + a[3] * d[3][c] for c in range(5)
        ]
    if grad is None:
        return value, None
    q = []
    for i in range(4):
        t = grad[0] * d[i][0]
        for c in range(1, 5):
            t = t + grad[c] * d[i][c]
        q.append(t * (1.0 / 6.0))
    dw = [5.0 * q[1] - 2.0 * q[0], q[1] + 2.0 * q[2], 4.0 * q[2] - q[3]]
    mid = w[0] * dw[0] + w[1] * dw[1] + w[2] * dw[2]
    ds = [(dw[k] - mid) * inv_sum * slopes[k] for k in range(3)]
    e = [0.0, 0.0, 0.0]
    for j in range(HID):
        dh = scal[W_OUT + 3 * j] * ds[0]
        dh = dh + scal[W_OUT + 3 * j + 1] * ds[1]
        dh = dh + scal[W_OUT + 3 * j + 2] * ds[2]
        dpre = dh * (1.0 - hidden[j] * hidden[j])
        e = [e[k] + scal[W_IN + HID * k + j] * dpre for k in range(3)]
    e = [0.2 * v for v in e]
    cells = [[], [], [], [], []]
    for c in range(5):
        d1, d2, d3, d4 = d[0][c], d[1][c], d[2][c], d[3][c]
        r, inv, gc = ratios[c], inverses[c], grad[c]
        m = e[0] * r[0] + e[1] * r[1] + e[2] * r[2]
        g0, g1, g2 = (e[0] - m) * inv, (e[1] - m) * inv, (e[2] - m) * inv
        dd1 = a[0] * gc + g0 * (8.0 * d1 - 11.0 * d2)
        dd2 = a[1] * gc + g0 * (20.0 * d2 - 11.0 * d1) + g1 * (8.0 * d2 - 5.0 * d3)
        dd3 = a[2] * gc + g1 * (8.0 * d3 - 5.0 * d2) + g2 * (20.0 * d3 - 11.0 * d4)
        dd4 = a[3] * gc + g2 * (8.0 * d4 - 11.0 * d3)
        cells[0].append(-dd1)
        cells[1].append(dd1 - dd2)
        cells[2].append(dd2 - dd3 + gc)
        cells[3].append(dd3 - dd4)
        cells[4].append(dd4)
    return value, cells


def build_lines(scal, q, zlo, zhi, ylo, yhi, xin, uz, uy, ux):
    for c in range(5):
        uz[c, 0:30] = zlo[c, 0:30]
        uz[c, 30:120] = q[c, 0:OWN]
        uz[c, 120:150] = zhi[c, 0:30]
        uz[c, 150:160] = jnp.ones((10, LANES), jnp.float32)
        for z in range(CZ):
            uy[c, pl.ds(27 + z, CY, stride=CZ), :] = q[c, z * CY : (z + 1) * CY]
        flip = -1.0 if c == 2 else 1.0
        for g in range(3):
            low = scal[0] * flip * uy[c, (5 - g) * 9 : (6 - g) * 9] + scal[1] * uy[c, 27:36]
            uy[c, g * 9 : g * 9 + 9] = low + scal[2] * ylo[c, g * 9 : g * 9 + 9]
            high = scal[3] * flip * uy[c, (12 - g) * 9 : (13 - g) * 9] + scal[4] * uy[c, 108:117]
            uy[c, (13 + g) * 9 : (14 + g) * 9] = high + scal[5] * yhi[c, g * 9 : g * 9 + 9]
        uy[c, 144:160] = jnp.ones((16, LANES), jnp.float32)
        flip = -1.0 if c == 1 else 1.0
        own = q[c]
        partner = xin[c]
        value = own * lane_mask(ROWS, 3, 125)
        low = scal[8] * roll(partner, 6)
        high = scal[11] * roll(partner, 122)
        value = value + lane_mask(ROWS, 0, 3) * low + lane_mask(ROWS, 125, 128) * high
        for g in range(3):
            at_low = lane_mask(ROWS, g, g + 1)
            value = value + at_low * (
                scal[6] * flip * roll(own, -(5 - 2 * g)) + scal[7] * roll(own, g - 3)
            )
            at_high = lane_mask(ROWS, 125 + g, 126 + g)
            value = value + at_high * (
                scal[9] * flip * roll(own, 1 + 2 * g) + scal[10] * roll(own, 1 + g)
            )
        ux[c] = value


def cell_loop(name, u, plus, minus, smooth, rows):
    def body(i, carry):
        at = pl.ds(pl.multiple_of(i * 16, 16), 16)
        cells = [u[c, at, :] for c in range(5)]
        flux, sv = cell_terms(COMP[name], cells)
        for c in range(5):
            plus[c, at, :] = 0.5 * flux[c] + cells[c]
            minus[c, at, :] = 0.5 * flux[c] - cells[c]
        if smooth is not None:
            for c in range(4):
                smooth[c, at, :] = sv[c]
        return carry

    lax.fori_loop(0, rows // 16, body, 0)


def spread_rows(name, plus, minus, diffs, base):
    p = PITCH[name]
    at_plus, at_minus, count = FACE_ROWS[name]
    for c in range(5):
        for start, size in ((0, 56), (56, 48)):
            f = [plus[c, start + k * p : start + k * p + size] for k in range(5)]
            for i in range(4):
                diffs[i, c, at_plus + start : at_plus + start + size] = f[i + 1] - f[i]
            middle = f[2]
            f = [minus[c, start + k * p : start + k * p + size] for k in range(1, 6)]
            for i in range(4):
                diffs[i, c, at_minus + start : at_minus + start + size] = f[3 - i] - f[4 - i]
            if base is not None:
                base[c, at_plus // 2 + start : at_plus // 2 + start + size] = middle + f[2]


def spread_lanes(plus, minus, diffs, base):
    at_plus, at_minus, count = FACE_ROWS["x"]
    for c in range(5):
        for start in (0, 48):
            v = plus[c, start : start + 48]
            diff = roll(v, -1) - v
            for i in range(4):
                diffs[i, c, at_plus + start : at_plus + start + 48] = roll(diff, -i)
            m = minus[c, start : start + 48]
            diff = m - roll(m, -1)
            for i in range(4):
                diffs[i, c, at_minus + start : at_minus + start + 48] = roll(diff, i - 4)
            if base is not None:
                base[c, at_plus // 2 + start : at_plus // 2 + start + 48] = roll(v, -2) + roll(
                    m, -3
                )


def lap_rows(name, smooth, out):
    p = PITCH[name]
    out[0] = jnp.zeros((ROWS, LANES), jnp.float32)
    for c in range(4):
        coef = 0.02 if c < 3 else 0.03
        s = [smooth[c, k * p : k * p + OWN] for k in (2, 3, 4)]
        out[c + 1, 0:OWN] = coef * (s[2] - 2.0 * s[1] + s[0])


def gather_grad(prev, coef, scale, own, zlo, zhi, ylo, yhi, xin, total, grad):
    for c in range(5):
        x = lane_mask(ROWS, 122, 125) * roll(xin[c], 122) + lane_mask(ROWS, 3, 6) * roll(xin[c], 6)
        total[c] = coef * prev[c] + own[c] + x
        total[c, 0:30] = total[c, 0:30] + zlo[c, 0:30]
        total[c, 60:90] = total[c, 60:90] + zhi[c, 0:30]
        for z in range(CZ):
            low = z * CY
            total[c, low : low + 3] = total[c, low : low + 3] + ylo[c, pl.ds(z, 3, stride=CZ), :]
            total[c, low + 7 : low + 10] = (
                total[c, low + 7 : low + 10] + yhi[c, pl.ds(z, 3, stride=CZ), :]
            )
        if grad is not None:
            grad[c] = scale * total[c]


def grad_faces(grad, gz, gy, dface):
    for c in range(5):
        gz[c] = jnp.zeros((GPAD, LANES), jnp.float32)
        gy[c] = jnp.zeros((GPAD, LANES), jnp.float32)
        gz[c, 40 : 40 + OWN] = grad[c, 0:OWN]
        for z in range(CZ):
            gy[c, pl.ds(36 + z, CY, stride=CZ), :] = grad[c, z * CY : (z + 1) * CY]
        dz = gz[c, 40:144] - gz[c, 30:134]
        dy = gy[c, 36:140] - gy[c, 27:131]
        g = grad[c]
        dx = roll(g, -3) - roll(g, -2)
        dface[c, 0:104] = dz
        dface[c, 104:208] = dz
        dface[c, 208:312] = dy
        dface[c, 312:416] = dy
        dface[c, 416:512] = dx
        dface[c, 512:608] = dx


def pull_rows(name, dcell, plus, minus, gpad, u, out):
    p = PITCH[name]
    at_plus, at_minus, count = FACE_ROWS[name]
    for c in range(5):
        plus[c] = jnp.zeros((CELLS, LANES), jnp.float32)
        minus[c] = jnp.zeros((CELLS, LANES), jnp.float32)
        for k in range(5):
            low = k * p
            plus[c, low : low + 104] = (
                plus[c, low : low + 104] + dcell[k, c, at_plus : at_plus + 104]
            )
            low = (5 - k) * p
            minus[c, low : low + 104] = (
                minus[c, low : low + 104] + dcell[k, c, at_minus : at_minus + 104]
            )
        if c > 0:
            coef = 0.02 if c < 4 else 0.03
            g = [gpad[c, k * p : k * p + CELLS] for k in range(3)]
            out[c] = coef * (g[0] - 2.0 * g[1] + g[2])
    pull_cells(name, plus, minus, u, out, CELLS)


def pull_lanes(dcell, plus, minus, grad, u, out):
    at_plus, at_minus, count = FACE_ROWS["x"]
    for c in range(5):
        sp = dcell[0, c, at_plus : at_plus + ROWS]
        sm = roll(dcell[0, c, at_minus : at_minus + ROWS], 5)
        for k in range(1, 5):
            sp = sp + roll(dcell[k, c, at_plus : at_plus + ROWS], k)
            sm = sm + roll(dcell[k, c, at_minus : at_minus + ROWS], 5 - k)
        plus[c, 0:ROWS] = sp
        minus[c, 0:ROWS] = sm
        if c > 0:
            coef = 0.02 if c < 4 else 0.03
            g = grad[c]
            out[c, 0:ROWS] = coef * (roll(g, 1) - 2.0 * g + roll(g, -1))
    pull_cells("x", plus, minus, u, out, ROWS)


def pull_cells(name, plus, minus, u, out, rows):
    def body(i, carry):
        at = pl.ds(pl.multiple_of(i * 16, 16), 16)
        cells = [u[c, at, :] for c in range(5)]
        dp = [plus[c, at, :] for c in range(5)]
        dm = [minus[c, at, :] for c in range(5)]
        dsv = [out[c, at, :] for c in range(1, 5)]
        unused, back = jax.vjp(functools.partial(cell_terms, COMP[name]), cells)
        (du,) = back(([0.5 * (dp[c] + dm[c]) for c in range(5)], dsv))
        for c in range(5):
            out[c, at, :] = du[c] + dp[c] - dm[c]
        return carry

    lax.fori_loop(0, rows // 16, body, 0)


def section(mode, consts, scal, q, halo, first, prev, own_in, halo_grad, state_out, sends, total,
            own_out, grad_sends, dx, work):
    zlo, zhi, ylo, yhi, xin = halo
    uz, uy, ux, plus, minus, smooth, diffs, base, tend_z, tend_y, tend_x, corr = work[:12]
    grad, gz, gy, dface, dcell, dline, dline_y = work[12:]
    if mode == "back":
        base = None
    if mode != "fwd":
        dzlo, dzhi, dylo, dyhi = grad_sends

    build_lines(scal, q, zlo, zhi, ylo, yhi, xin, uz, uy, ux)
    wants = mode != "back"
    lap = smooth if wants else None
    for name, u, tend in (("z", uz, "tz"), ("y", uy, "ty")):
        cell_loop(name, u, plus, minus, lap, CELLS)
        spread_rows(name, plus, minus, diffs, base)
        if wants:
            lap_rows(name, smooth, tend_z if name == "z" else tend_y)
    cell_loop("x", ux, plus, minus, lap, ROWS)
    spread_lanes(plus, minus, diffs, base)
    if wants:
        tend_x[0] = jnp.zeros((ROWS, LANES), jnp.float32)
        for c in range(4):
            s = smooth[c, 0:ROWS]
            coef = 0.02 if c < 3 else 0.03
            tend_x[c + 1] = coef * (roll(s, 1) - 2.0 * s + roll(s, -1))

    if mode == "both":
        for c in range(5):
            grad[c] = consts["scale"] * prev[c]
    if mode == "back":
        gather_grad(prev, consts["coef"], consts["scale"], own_in, *halo_grad(), total, grad)
    if mode != "fwd":
        grad_faces(grad, gz, gy, dface)

    def body(i, carry):
        at = pl.ds(pl.multiple_of(i * 16, 16), 16)
        d = [[diffs[k, c, at, :] for c in range(5)] for k in range(4)]
        g = None if mode == "fwd" else [dface[c, at, :] for c in range(5)]
        value, cells = weno_unit(d, scal, g, wants)
        if wants:
            for c in range(5):
                corr[c, at, :] = value[c]
        if cells is not None:
            for k in range(5):
                for c in range(5):
                    dcell[k, c, at, :] = cells[k][c]
        return carry

    lax.fori_loop(0, FACES // 16, body, 0)

    if wants:
        inside = lane_mask(OWN, 3, 125)
        for c in range(5):
            fz = base[c, 0:104] + corr[c, 0:104] + corr[c, 104:208]
            base[c, 0:104] = fz
            fy = base[c, 104:208] + corr[c, 208:312] + corr[c, 312:416]
            base[c, 104:208] = fy
            fx = base[c, 208:304] + corr[c, 416:512] + corr[c, 512:608]
            tend_z[c, 0:OWN] = tend_z[c, 0:OWN] + base[c, 0:OWN] - base[c, 10 : 10 + OWN]
            tend_y[c, 0:OWN] = tend_y[c, 0:OWN] + base[c, 104 : 104 + OWN] - base[c, 113 : 113 + OWN]
            tend_x[c] = tend_x[c] + roll(fx, 3) - roll(fx, 2)
            for z in range(CZ):
                low = z * CY
                tend_z[c, low : low + CY] = (
                    tend_z[c, low : low + CY] + tend_y[c, pl.ds(z, CY, stride=CZ), :]
                )
            t = (tend_z[c, 0:OWN] + tend_x[c, 0:OWN]) * (inside * DT)
            state_out[c, 0:OWN] = (
                consts["first"] * first[c, 0:OWN] + consts["last"] * (q[c, 0:OWN] + t)
            )
            state_out[c, OWN:ROWS] = jnp.ones((ROWS - OWN, LANES), jnp.float32)
        if mode == "fwd":
            cut_edges(state_out, sends)

    if mode != "fwd":
        pull_rows("z", dcell, plus, minus, gz, uz, dline)
        for c in range(5):
            own_out[c, 0:OWN] = dline[c, 30:120]
            own_out[c, OWN:ROWS] = jnp.zeros((ROWS - OWN, LANES), jnp.float32)
            dzlo[c, 0:30] = dline[c, 0:30]
            dzhi[c, 0:30] = dline[c, 120:150]
        pull_rows("y", dcell, plus, minus, gy, uy, dline_y)
        for c in range(5):
            flip = -1.0 if c == 2 else 1.0
            dylo[c, 0:27] = scal[2] * dline_y[c, 0:27]
            dyhi[c, 0:27] = scal[5] * dline_y[c, 117:144]
            for g in range(3):
                low = dline_y[c, g * 9 : g * 9 + 9]
                high = dline_y[c, (13 + g) * 9 : (14 + g) * 9]
                at = (5 - g) * 9
                dline_y[c, at : at + 9] = dline_y[c, at : at + 9] + scal[0] * flip * low
                dline_y[c, 27:36] = dline_y[c, 27:36] + scal[1] * low
                at = (12 - g) * 9
                dline_y[c, at : at + 9] = dline_y[c, at : at + 9] + scal[3] * flip * high
                dline_y[c, 108:117] = dline_y[c, 108:117] + scal[4] * high
            for z in range(CZ):
                low = z * CY
                own_out[c, low : low + CY] = (
                    own_out[c, low : low + CY] + dline_y[c, pl.ds(27 + z, CY, stride=CZ), :]
                )
        pull_lanes(dcell, plus, minus, grad, ux, dline)
        rows_on = jnp.where(
            lax.broadcasted_iota(jnp.int32, (ROWS, LANES), 0) < OWN, 1.0, 0.0
        ).astype(jnp.float32)
        for c in range(5):
            flip = -1.0 if c == 1 else 1.0
            v = dline[c, 0:ROWS] * rows_on
            dx[c] = v * (
                lane_mask(ROWS, 0, 3) * scal[8] + lane_mask(ROWS, 125, 128) * scal[11]
            )
            acc = v + own_out[c]
            for g in range(3):
                low = v * lane_mask(ROWS, g, g + 1)
                high = v * lane_mask(ROWS, 125 + g, 126 + g)
                acc = acc + scal[6] * flip * roll(low, 5 - 2 * g) + scal[7] * roll(low, 3 - g)
                acc = acc + scal[9] * flip * roll(high, -1 - 2 * g) + scal[10] * roll(high, -1 - g)
            own_out[c] = acc * lane_mask(ROWS, 3, 125)


FULL = (5, ROWS, LANES)
EDGE = (5, 32, LANES)
LINE = (5, CELLS, LANES)
GLINE = (5, GPAD, LANES)
WORK = [LINE, LINE, FULL, LINE, LINE, (4, CELLS, LANES), (4, 5, FACES, LANES)]
WORK += [(5, 304, LANES), FULL, FULL, FULL, (5, FACES, LANES)]
WORK += [FULL, GLINE, GLINE, (5, FACES, LANES), (5, 5, FACES, LANES), LINE, LINE]


def cut_edges(field, sends):
    szlo, szhi, sylo, syhi = sends
    for c in range(5):
        szlo[c, 0:30] = field[c, 0:30]
        szhi[c, 0:30] = field[c, 60:90]
        for z in range(CZ):
            low = z * CY
            sylo[c, pl.ds(z, 3, stride=CZ), :] = field[c, low : low + 3]
            syhi[c, pl.ds(z, 3, stride=CZ), :] = field[c, low + 7 : low + 10]


def step_kernel(sizes, scal, state, cot, new_out, grad_out, one, two, grad_two, grad_one, own, dx,
                sends, takes, xtakes, send_sem, recv_sem, *work):
    peers = []
    for axis in ("gz", "gy"):
        place, count = lax.axis_index(axis), sizes[axis]
        peers.append({axis: lax.rem(place + count - 1, count)})
        peers.append({axis: lax.rem(place + 1, count)})
    peers.append({"gx": 1 - lax.axis_index("gx")})
    mesh_id = pl.DeviceIdType.MESH

    barrier = pltpu.get_barrier_semaphore()
    for peer in peers:
        pl.semaphore_signal(barrier, inc=1, device_id=peer, device_id_type=mesh_id)
    pl.semaphore_wait(barrier, len(peers))

    flights = {}

    def send_to(turn, full):
        flights[turn] = []
        for i, peer in enumerate(peers):
            copy = pltpu.make_async_remote_copy(
                src_ref=full if i == 4 else sends.at[turn, i],
                dst_ref=xtakes.at[turn] if i == 4 else takes.at[turn, i ^ 1],
                send_sem=send_sem.at[turn, i],
                recv_sem=recv_sem.at[turn, i],
                device_id=peer,
                device_id_type=mesh_id,
            )
            copy.start()
            flights[turn].append(copy)

    def arrive(turn):
        for copy in flights[turn]:
            copy.wait_recv()
        return halo(turn)

    def halo(turn):
        return [takes.at[turn, i] for i in range(4)] + [xtakes.at[turn]]

    def edges(turn):
        return [sends.at[turn, i] for i in range(4)]

    cut_edges(state, edges(0))
    send_to(0, state)
    section("fwd", dict(first=0.0, last=1.0), scal, state, arrive(0), state, None, None, None,
            one, edges(1), None, None, None, None, work)
    send_to(1, one)
    section("fwd", dict(first=0.75, last=0.25), scal, one, arrive(1), state, None, None, None,
            two, edges(2), None, None, None, None, work)
    send_to(2, two)
    section("both", dict(first=1.0 / 3.0, last=2.0 / 3.0, scale=DT * 2.0 / 3.0), scal, two,
            arrive(2), state, cot, None, None, new_out, None, None, own, edges(3), dx.at[0], work)
    send_to(3, dx.at[0])
    section("back", dict(coef=2.0 / 3.0, scale=0.25 * DT), scal, one, halo(1), None, cot, own,
            lambda: arrive(3), None, None, grad_two, own, edges(4), dx.at[1], work)
    send_to(4, dx.at[1])
    section("back", dict(coef=0.25, scale=DT), scal, state, halo(0), None, grad_two, own,
            lambda: arrive(4), None, None, grad_one, own, edges(5), dx.at[2], work)
    send_to(5, dx.at[2])
    for c in range(5):
        grad_one[c] = grad_one[c] + 0.75 * grad_two[c] + (1.0 / 3.0) * cot[c]
    gather_grad(grad_one, 1.0, None, own, *arrive(5), grad_out, None)
    for turn in range(6):
        for copy in flights[turn]:
            copy.wait_send()


def flat(field, fill):
    lanes = jnp.pad(
        field, ((0, 0), (0, 0), (0, 0), (3, 3)), constant_values=fill
    ).reshape(5, OWN, LANES)
    return jnp.pad(lanes, ((0, 0), (0, ROWS - OWN), (0, 0)), constant_values=fill)


def unflat(field):
    return field[:, :OWN].reshape(5, CZ, CY, LANES)[..., 3 : 3 + CX]


def run_step(scal, state, cot):
    shape = jax.ShapeDtypeStruct(FULL, jnp.float32)
    vmem = pl.BlockSpec(memory_space=pltpu.VMEM)
    scratch = [FULL] * 5 + [(3,) + FULL, (6, 4) + EDGE, (6, 4) + EDGE, (6,) + FULL]
    sizes = {axis: lax.axis_size(axis) for axis in ("gz", "gy")}
    return pl.pallas_call(
        functools.partial(step_kernel, sizes),
        out_shape=[shape, shape],
        in_specs=[pl.BlockSpec(memory_space=pltpu.SMEM), vmem, vmem],
        out_specs=[vmem, vmem],
        scratch_shapes=[pltpu.VMEM(s, jnp.float32) for s in scratch]
        + [pltpu.SemaphoreType.DMA((6, 5))] * 2
        + [pltpu.VMEM(s, jnp.float32) for s in WORK],
        compiler_params=pltpu.CompilerParams(
            vmem_limit_bytes=56 * 1024 * 1024, collective_id=0, has_side_effects=True
        ),
        name="step",
    )(scal, state, cot)


def on_device(density, momentum, energy, cotangent, bc_codes, weight_in, weight_out):
    state = flat(jnp.concatenate([density[None], momentum, energy[None]], 0), 1.0)
    cot = flat(cotangent, 0.0)
    y_place = lax.axis_index("gy")
    x_place = lax.axis_index("gx")
    edges = jnp.stack(
        [
            y_place == 0,
            y_place == lax.axis_size("gy") - 1,
            x_place == 0,
            x_place == lax.axis_size("gx") - 1,
        ]
    ).astype(jnp.float32)
    wall = (bc_codes == 0).astype(jnp.float32)
    sides = jnp.stack([edges * wall, edges * (1.0 - wall), 1.0 - edges], 1).reshape(12)
    scal = jnp.concatenate([sides, weight_in.reshape(-1), weight_out.reshape(-1)])

    new_state, total = run_step(scal, state, cot)
    return (unflat(new_state), unflat(total))


def solution(mesh):
    in_specs = (
        P(("groups", "gz"), "gy", "gx"),
        P(None, ("groups", "gz"), "gy", "gx"),
        P(("groups", "gz"), "gy", "gx"),
        P(None, ("groups", "gz"), "gy", "gx"),
        P("groups"),
        P(),
        P(),
    )
    out_specs = (P(None, ("groups", "gz"), "gy", "gx"), P(None, ("groups", "gz"), "gy", "gx"))
    return jax.shard_map(
        on_device, mesh=mesh, in_specs=in_specs, out_specs=out_specs, check_vma=False
    )
```
